512 devices in a mesh: dp: 16 (over y, x), cent: 32 (over z, core).
Axes of the slice: x: 4, y: 4, z: 16, core: 2. Of those that a mesh axis runs over, the one named last changes fastest.
Arguments:
- points: float32 [524288, 128], P(('dp', 'cent')), may hold values from -6 to 6
- row_weight: float32 [524288], P(('dp', 'cent')), may hold values from 0.25 to 4
- labels: int32 [2, 524288], P(None, ('dp', 'cent')), may hold values from 0 to 32767, as said below
- centroids: float32 [32768, 128], P('cent'), may hold values from -6 to 6
- prior_prec: float32 [128], replicated, may hold values from 0.5 to 8
Outputs:
- centroids_new: float32 [32768, 128], P('cent')
The draws below stay inside these ranges and needn't reach their ends.
Inputs may be any that keep to these rules, and one draw needn't show every extreme that they name: Within the rows of one device, at most 64 rows in one step have labels in the same aligned range of 1024 centroids, and in every step some range receives exactly 64 of that device's rows.
All inputs are finite; a program needn't handle non-finite values.
Results may differ from the reference program's by a relative error of at most 0.0001.
Values sent between devices are 32-bit elements; how exact they have to be, the bound alone decides.
No kernel may reach another device: no remote copies, remote signals or barrier semaphores. Data moves between devices by JAX's collectives and lax.ppermute only.
A program may use at most 64 MiB of HBM per device.

```python
import math
import jax
import jax.numpy as jnp

D = 128
CENT_DEV = 1024
ROWS_DEV = 1024
ITERS = 3
STEPS = 2
CENTS = 32768
ROWS = 524288
N_DP = 16
N_CENT = 32


def draw_labels(key, part):
    blocks = N_DP * N_CENT
    capacity = 2 * ROWS_DEV // N_CENT

    def one_section(section_key):
        first_key, second_key = jax.random.split(section_key)
        heat = 2 ** jax.random.randint(first_key, (N_CENT,), 0, 5)
        block_keys = jax.random.split(second_key, blocks)

        def one_block(block_key):
            key_order, key_jitter, key_local, key_shuffle = jax.random.split(block_key, 4)
            order = jax.random.permutation(key_order, N_CENT)
            leader = order[0::2]
            partner = order[1::2]
            heat_one = heat[leader]
            heat_two = heat[partner]
            jitter = jax.random.randint(key_jitter, (N_CENT // 2,), -(capacity // 8), capacity // 8 + 1)
            share = jnp.clip(capacity * heat_one // (heat_one + heat_two) + jitter, 0, capacity)
            share = share.at[0].set(capacity)
            counts = jnp.zeros((N_CENT,), jnp.int32).at[leader].set(share).at[partner].set(capacity - share)
            ends = jnp.cumsum(counts)
            slots = jnp.arange(ROWS_DEV, dtype=jnp.int32)
            target = jnp.searchsorted(ends, slots, side='right').astype(jnp.int32)
            local = jax.random.randint(key_local, (ROWS_DEV,), 0, CENT_DEV)
            chosen = target * CENT_DEV + local
            return jax.random.permutation(key_shuffle, chosen)
        return jax.vmap(one_block)(block_keys).reshape(-1)
    return jax.vmap(one_section)(jax.random.split(key, STEPS)).astype(jnp.int32)


def block_scale(stream_key, dims, shards, low, largest):
    loudness, own = 1.0, jax.random.fold_in(stream_key, 6)
    for dim, shards_of in shards:
        draws = jnp.exp(jax.random.uniform(jax.random.fold_in(own, dim), (shards_of,), jnp.float32, low / len(shards), largest / len(shards)))
        loudness = loudness * jnp.repeat(draws, dims[dim] // shards_of).reshape([-1 if axis == dim else 1 for axis in range(len(dims))])
    return loudness


def centred(key, shape, scale, most, cuts=(), kind=jnp.bfloat16):
    entries = jax.random.normal(key, shape, jnp.float32) * scale
    if len(cuts) > 0:
        entries = block_scale(key, shape, cuts, -0.22, 0.18) * entries
    return jnp.clip(entries, min=-most, max=most).astype(kind)


def setup_inputs(seed: int = 0) -> dict:
    splits = jax.random.split(jax.random.key(seed), 6)
    return {
        "points": centred(splits[0], (ROWS, D), 1.0, 6.0, ((0, 512),), jnp.float32),
        "row_weight": jnp.clip(jnp.exp(math.log(4.0) - 2.7725887 * jax.random.uniform(splits[1], (ROWS,), jnp.float32) ** block_scale(splits[1], (ROWS,), ((0, 512),), -0.2, 0.2)), 0.25, 4.0),
        "labels": draw_labels(jax.random.fold_in(splits[5], 71), 0),
        "centroids": centred(splits[3], (CENTS, D), 1.0, 6.0, ((0, 32),), jnp.float32),
        "prior_prec": jnp.clip(jnp.exp(jax.random.uniform(splits[4], (D,), jnp.float32, math.log(0.5), math.log(8.0))), 0.5, 8.0),
    }


parallel_ratio = 4.0
tiny = 1e-6


def reference(points, row_weight, labels, centroids, prior_prec):
    total = centroids.shape[0]
    power = jnp.mean(points * points, axis=1)
    coupling = row_weight * (parallel_ratio - 1.0) / (points.shape[1] * (power + tiny))
    weighted = row_weight[:, None] * points
    current = centroids
    for section in range(STEPS):
        owner = labels[section]
        rhs = prior_prec[None, :] * current + parallel_ratio * jax.ops.segment_sum(weighted, owner, num_segments=total)

        def apply(vector):
            picked = jnp.take(vector, owner, axis=0)
            along = jnp.sum(points * picked, axis=1) * coupling
            term = row_weight[:, None] * picked + along[:, None] * points
            return prior_prec[None, :] * vector + jax.ops.segment_sum(term, owner, num_segments=total)

        solution = jnp.zeros_like(rhs)
        residual = rhs
        direction = rhs
        norm_now = jnp.sum(residual * residual, axis=1)
        for turn in range(ITERS):
            image = apply(direction)
            alpha = norm_now / (jnp.sum(direction * image, axis=1) + tiny)
            solution = solution + alpha[:, None] * direction
            residual = residual - alpha[:, None] * image
            norm_next = jnp.sum(residual * residual, axis=1)
            direction = residual + (norm_next / (norm_now + tiny))[:, None] * direction
            norm_now = norm_next
        current = solution
    return current
```

```python
import functools

import jax
import jax.numpy as jnp
from jax import lax
from jax.experimental import pallas as pl
from jax.experimental.pallas import tpu as pltpu
from jax.sharding import PartitionSpec as P

ITERS = 3
CAP = 192
PITCH = CAP + 8
LANES = 128
LIMIT = 48 * 1024 * 1024

parallel_ratio = 4.0
tiny = 1e-06


def _dot(a, b):
    return jnp.dot(a, b, preferred_element_type=jnp.float32)


def _dot_t(a, b):
    return lax.dot_general(a, b, (((1,), (1,)), ((), ())), preferred_element_type=jnp.float32)


def _halves(x):
    high = x.astype(jnp.bfloat16)
    low = (x - high.astype(jnp.float32)).astype(jnp.bfloat16)
    return high, low


def _iota(shape, dim):
    return lax.broadcasted_iota(jnp.int32, shape, dim)


def _upper():
    return (_iota((LANES, LANES), 0) <= _iota((LANES, LANES), 1)).astype(jnp.bfloat16)


def _places(marks, groups):
    within = _dot(jnp.concatenate(marks, axis=0).astype(jnp.bfloat16), _upper())
    before = jnp.zeros((groups, 1), jnp.float32)
    places = []
    for k, mark in enumerate(marks):
        part = within[k * groups : (k + 1) * groups]
        places.append(jnp.sum(mark * (part + (before - 1.0)), axis=0, keepdims=True))
        before = before + part[:, LANES - 1 :]
    return places, before


def _pack_kernel(peers, slots, held, odd_ref, x_ref, w_ref, t_ref, out_ref):
    rows = x_ref.shape[0]
    steps = t_ref.shape[0]
    high, low = _halves(x_ref[...])
    both = jnp.concatenate([high, low], axis=1)
    w_high, w_low = _halves(w_ref[...])
    first = (_iota((peers, 2 * slots), 1) < slots).astype(jnp.int32)
    for step in range(steps):
        label = t_ref[step : step + 1, :]
        target = label // held
        local = label - target * held
        marks = (_iota((peers, rows), 0) == target).astype(jnp.float32)
        chunks = [marks[:, k : k + LANES] for k in range(0, rows, LANES)]
        places, _ = _places(chunks, peers)
        place = jnp.concatenate(places, axis=1).astype(jnp.int32)
        l_high, l_low = _halves(local.astype(jnp.float32))
        values = jnp.concatenate(
            [marks * v.astype(jnp.float32) for v in (w_high, w_low, l_high, l_low)], axis=0
        ).astype(jnp.bfloat16)
        at = ((_iota((2 * slots, rows), 0) % slots) == place).astype(jnp.bfloat16)
        notes = _dot_t(values, at)
        weight = notes[:peers] + notes[peers : 2 * peers]
        index = notes[2 * peers : 3 * peers] + notes[3 * peers :]
        notes = jnp.where(first != odd_ref[0], weight, index)
        slot = target * slots + place
        block = 8
        for b in range(0, peers, block):
            take = (_iota((block * slots, rows), 0) + b * slots == slot).astype(jnp.bfloat16)
            got = _dot(take, both)
            got = got[:, :LANES] + got[:, LANES:]
            for t in range(block):
                base = ((b + t) * steps + step) * (slots + 1)
                out_ref[base : base + slots, :] = got[t * slots : (t + 1) * slots]
                out_ref[base + slots : base + slots + 1, :] = notes[b + t : b + t + 1]


def _pack(points, weight, labels, odd, peers, slots, held):
    return pl.pallas_call(
        functools.partial(_pack_kernel, peers, slots, held),
        out_shape=jax.ShapeDtypeStruct((peers * labels.shape[0] * (slots + 1), LANES), jnp.float32),
        in_specs=[pl.BlockSpec(memory_space=pltpu.SMEM)] + [pl.BlockSpec(memory_space=pltpu.VMEM)] * 3,
        compiler_params=pltpu.CompilerParams(vmem_limit_bytes=LIMIT),
        name="pack",
    )(odd, points, weight, labels)


def _repack_kernel(peers, slots, held, groups, steps, x_ref, out_ref, even_ref, odd_ref, both_ref):
    pairs = peers // 2
    rows = peers * slots
    per = held // groups
    first = _iota((pairs, LANES), 1) < slots
    for step in range(steps):
        for b in range(peers):
            base = (b * steps + step) * (slots + 1)
            high, low = _halves(x_ref[base : base + slots, :])
            both_ref[b * slots : (b + 1) * slots, :LANES] = high
            both_ref[b * slots : (b + 1) * slots, LANES:] = low
            note_ref = odd_ref if b % 2 else even_ref
            note_ref[b // 2 : b // 2 + 1, :] = x_ref[base + slots : base + slots + 1, :]
        even, odd = even_ref[...], odd_ref[...]
        weight = jnp.where(first, even, odd)
        local = pltpu.roll(jnp.where(first, odd, even), slots, 1).astype(jnp.int32)
        owner = jnp.where(weight > 0.0, local // per, -1)
        index = (local % per).astype(jnp.float32)
        marks = [
            (_iota((groups, LANES), 0) == owner[k : k + 1]).astype(jnp.float32) for k in range(pairs)
        ]
        places, sizes = _places(marks, groups)
        flag = jnp.max(sizes, axis=0, keepdims=True) > CAP
        flag = jnp.where(flag, jnp.ones((1, LANES), jnp.float32), 0.0)
        place = jnp.concatenate(places, axis=1).astype(jnp.int32)
        owner = jnp.concatenate([owner[k : k + 1] for k in range(pairs)], axis=1)
        fits = (owner >= 0) & (place < CAP)
        place = jnp.where(fits, place, -1)
        slot = jnp.where(fits, owner * PITCH + place, -1)
        w_high, w_low = _halves(weight)
        values = jnp.concatenate(
            [
                jnp.concatenate([marks[k] * v[k : k + 1] for k in range(pairs)], axis=1)
                for v in (w_high.astype(jnp.float32), w_low.astype(jnp.float32), index)
            ],
            axis=0,
        ).astype(jnp.bfloat16)
        at = (_iota((2 * LANES, rows), 0) == place).astype(jnp.bfloat16)
        notes = _dot_t(values, at)
        weight = notes[:groups] + notes[groups : 2 * groups]
        index = notes[2 * groups :]
        both = both_ref[...]
        for o in range(0, groups, 2):
            take = (_iota((2 * PITCH, rows), 0) + o * PITCH == slot).astype(jnp.bfloat16)
            got = _dot(take, both)
            got = got[:, :LANES] + got[:, LANES:]
            for half in range(2):
                base = ((o + half) * steps + step) * PITCH
                out_ref[base : base + PITCH, :] = got[half * PITCH : (half + 1) * PITCH]
                base = base + CAP
                own = slice(o + half, o + half + 1)
                out_ref[base : base + 1, :] = weight[own, :LANES]
                out_ref[base + 1 : base + 2, :] = weight[own, LANES:]
                out_ref[base + 2 : base + 3, :] = index[own, :LANES]
                out_ref[base + 3 : base + 4, :] = index[own, LANES:]
                out_ref[base + 4 : base + 5, :] = flag


def _repack(got, peers, slots, held, groups, steps):
    return pl.pallas_call(
        functools.partial(_repack_kernel, peers, slots, held, groups, steps),
        out_shape=jax.ShapeDtypeStruct((groups * steps * PITCH, LANES), jnp.float32),
        scratch_shapes=[
            pltpu.VMEM((peers // 2, LANES), jnp.float32),
            pltpu.VMEM((peers // 2, LANES), jnp.float32),
            pltpu.VMEM((peers * slots, 2 * LANES), jnp.bfloat16),
        ],
        compiler_params=pltpu.CompilerParams(vmem_limit_bytes=LIMIT),
        name="repack",
    )(got)


def _solve_kernel(groups, steps, x_ref, cur_ref, prior_ref, out_ref, flag_ref, high_ref, low_ref):
    wide = 2 * LANES
    per = cur_ref.shape[0]
    ones = jnp.ones((8, LANES), jnp.bfloat16)
    flag = jnp.zeros((1, LANES), jnp.float32)
    current = cur_ref[...]
    for step in range(steps):
        weights, indices, powers = [], [], []
        for s in range(groups):
            base = (s * steps + step) * PITCH
            rows = x_ref[base : base + CAP, :]
            rows = jnp.concatenate([rows, jnp.zeros((wide - CAP, LANES), jnp.float32)], axis=0)
            high, low = _halves(rows)
            high_ref[s * wide : (s + 1) * wide, :] = high
            low_ref[s * wide : (s + 1) * wide, :] = low
            square_high, square_low = _halves(rows * rows)
            powers.append((_dot_t(ones, square_high) + _dot_t(ones, square_low))[:1])
            notes = x_ref[base + CAP : base + PITCH, :]
            weights += [notes[0:1], notes[1:2]]
            indices += [notes[2:3], notes[3:4]]
            flag = jnp.maximum(flag, notes[4:5])
        weight = jnp.concatenate(weights, axis=1)
        index = jnp.concatenate(indices, axis=1).astype(jnp.int32)
        power = jnp.concatenate(powers, axis=1) * (1.0 / LANES)
        coupling = weight * (parallel_ratio - 1.0) / (LANES * (power + tiny))
        mine = _iota((per, groups * wide), 0) == index
        weighted = jnp.where(mine, weight, 0.0)
        coupled = jnp.where(mine, coupling, 0.0)
        weight_sum = jnp.sum(weighted, axis=1, keepdims=True)
        high, low = high_ref[...], low_ref[...]

        def gather_up(terms):
            a, b = _halves(terms)
            c = _dot(jnp.concatenate([a, b], axis=0), high)
            return c[:per] + c[per:] + _dot(a, low)

        def along(vector):
            a, b = _halves(vector)
            c = _dot_t(jnp.concatenate([a, b], axis=0), high)
            return c[:per] + c[per:] + _dot_t(a, low)

        diagonal = prior_ref[...] + weight_sum
        rhs = prior_ref[...] * current + parallel_ratio * gather_up(weighted)
        current = jnp.zeros_like(rhs)
        residual = rhs
        direction = rhs
        norm_now = jnp.sum(residual * residual, axis=1, keepdims=True)
        for turn in range(ITERS):
            image = diagonal * direction + gather_up(along(direction) * coupled)
            alpha = norm_now / (jnp.sum(direction * image, axis=1, keepdims=True) + tiny)
            current = current + alpha * direction
            if turn + 1 < ITERS:
                residual = residual - alpha * image
                norm_next = jnp.sum(residual * residual, axis=1, keepdims=True)
                direction = residual + (norm_next / (norm_now + tiny)) * direction
                norm_now = norm_next
    out_ref[...] = current
    flag_ref[...] = flag


def _solve(got, current, prior, groups, steps):
    rows = groups * 2 * LANES
    return pl.pallas_call(
        functools.partial(_solve_kernel, groups, steps),
        out_shape=(
            jax.ShapeDtypeStruct(current.shape, jnp.float32),
            jax.ShapeDtypeStruct((1, LANES), jnp.float32),
        ),
        scratch_shapes=[
            pltpu.VMEM((rows, LANES), jnp.bfloat16),
            pltpu.VMEM((rows, LANES), jnp.bfloat16),
        ],
        compiler_params=pltpu.CompilerParams(vmem_limit_bytes=LIMIT),
        name="solve",
    )(got, current, prior)


def row_terms(vector, got_points, got_weight, got_local, coupling, held):
    picked = jnp.take(vector, got_local, axis=0)
    along = jnp.sum(got_points * picked, axis=1) * coupling
    term = got_weight[:, None] * picked + along[:, None] * got_points
    return jax.ops.segment_sum(term, got_local, num_segments=held)


def dp_sum(x):
    groups = lax.axis_size("dp")
    parts = x.reshape(groups, -1, x.shape[1])
    parts = lax.all_to_all(parts, "dp", split_axis=0, concat_axis=0, tiled=True)
    spread = jnp.broadcast_to(jnp.sum(parts, axis=0)[None], parts.shape)
    return lax.all_to_all(spread, "dp", split_axis=0, concat_axis=0, tiled=True).reshape(x.shape)


def solve_whole(got_points, got_weight, got_local, coupling, current, prior_prec, held):
    data = jax.ops.segment_sum(got_weight[:, None] * got_points, got_local, num_segments=held)
    rhs = prior_prec[None, :] * current + parallel_ratio * dp_sum(data)
    solution = jnp.zeros_like(rhs)
    residual = rhs
    direction = rhs
    norm_now = jnp.sum(residual * residual, axis=1)
    for turn in range(ITERS):
        partial_value = row_terms(direction, got_points, got_weight, got_local, coupling, held)
        image = prior_prec[None, :] * direction + dp_sum(partial_value)
        alpha = norm_now / (jnp.sum(direction * image, axis=1) + tiny)
        solution = solution + alpha[:, None] * direction
        residual = residual - alpha[:, None] * image
        norm_next = jnp.sum(residual * residual, axis=1)
        direction = residual + (norm_next / (norm_now + tiny))[:, None] * direction
        norm_now = norm_next
    return solution


def any_labels(got, centroids, prior_prec, peers, slots, steps):
    held, width = centroids.shape
    current = centroids
    got = got.reshape(peers, steps, slots + 1, width)
    for step in range(steps):
        block = got[:, step]
        points = block[:, :slots].reshape(-1, width)
        notes = block[:, slots].reshape(peers // 2, 2, 2, slots)
        weight = jnp.stack([notes[:, 0, 0], notes[:, 1, 1]], axis=1).reshape(-1)
        local = jnp.stack([notes[:, 0, 1], notes[:, 1, 0]], axis=1).reshape(-1).astype(jnp.int32)
        power = jnp.mean(points * points, axis=1)
        coupling = weight * (parallel_ratio - 1.0) / (width * (power + tiny))
        current = solve_whole(points, weight, local, coupling, current, prior_prec, held)
    return current


def per_device(points, row_weight, labels, centroids, prior_prec):
    peers = lax.axis_size("cent")
    groups = lax.axis_size("dp")
    held, width = centroids.shape
    slots = 2 * points.shape[0] // peers
    steps = labels.shape[0]
    per = held // groups
    odd = (lax.axis_index("cent") % 2).reshape(1)
    start = lax.axis_index("dp") * per
    sent = _pack(points, row_weight.reshape(1, -1), labels, odd, peers, slots, held)
    got = lax.all_to_all(
        sent.reshape(peers, steps * (slots + 1), 1, width), "cent", split_axis=0, concat_axis=0, tiled=True
    ).reshape(-1, width)
    again = _repack(got, peers, slots, held, groups, steps)
    again = lax.all_to_all(
        again.reshape(groups, steps * PITCH, width), "dp", split_axis=0, concat_axis=0, tiled=True
    ).reshape(-1, width)
    current = lax.dynamic_slice(centroids, (start, 0), (per, width))
    current, flag = _solve(again, current, prior_prec.reshape(1, -1), groups, steps)

    def summed(got, current):
        every = any_labels(got, centroids, prior_prec, peers, slots, steps)
        return lax.dynamic_slice(every, (start, 0), (per, width))

    current = lax.cond(flag[0, 0] > 0.0, summed, lambda got, current: current, got, current)
    spread = jnp.broadcast_to(current[None], (groups, per, width))
    spread = lax.all_to_all(spread, "dp", split_axis=0, concat_axis=0, tiled=True)
    return spread.reshape(held, width)


def solution(mesh):
    in_specs = (
        P(("dp", "cent"), None),
        P(("dp", "cent")),
        P(None, ("dp", "cent")),
        P("cent", None),
        P(),
    )
    out_specs = P("cent", None)
    return jax.shard_map(
        per_device, mesh=mesh, in_specs=in_specs, out_specs=out_specs, check_vma=False
    )
```

```python
import functools

import jax
import jax.numpy as jnp
from jax import lax
from jax.experimental import pallas as pl
from jax.experimental.pallas import tpu as pltpu
from jax.sharding import PartitionSpec as P

ITERS = 3
CAP = 192
PITCH = CAP + 8
LANES = 128
LIMIT = 48 * 1024 * 1024

parallel_ratio = 4.0
tiny = 1e-06


def _dot(a, b):
    return jnp.dot(a, b, preferred_element_type=jnp.float32)


def _dot_t(a, b):
    return lax.dot_general(a, b, (((1,), (1,)), ((), ())), preferred_element_type=jnp.float32)


def _halves(x):
    high = x.astype(jnp.bfloat16)
    low = (x - high.astype(jnp.float32)).astype(jnp.bfloat16)
    return high, low


def _iota(shape, dim):
    return lax.broadcasted_iota(jnp.int32, shape, dim)


def _upper():
    return (_iota((LANES, LANES), 0) <= _iota((LANES, LANES), 1)).astype(jnp.bfloat16)


def _places(marks, groups):
    within = _dot(jnp.concatenate(marks, axis=0).astype(jnp.bfloat16), _upper())
    before = jnp.zeros((groups, 1), jnp.float32)
    places = []
    for k, mark in enumerate(marks):
        part = within[k * groups : (k + 1) * groups]
        places.append(jnp.sum(mark * (part + (before - 1.0)), axis=0, keepdims=True))
        before = before + part[:, LANES - 1 :]
    return places, before


def _pack_kernel(peers, slots, held, odd_ref, x_ref, w_ref, t_ref, out_ref):
    rows = x_ref.shape[0]
    high, low = _halves(x_ref[...])
    both = jnp.concatenate([high, low], axis=1)
    w_high, w_low = _halves(w_ref[...])
    first = (_iota((peers, 2 * slots), 1) < slots).astype(jnp.int32)
    label = t_ref[...]
    target = label // held
    local = label - target * held
    marks = (_iota((peers, rows), 0) == target).astype(jnp.float32)
    chunks = [marks[:, k : k + LANES] for k in range(0, rows, LANES)]
    places, _ = _places(chunks, peers)
    place = jnp.concatenate(places, axis=1).astype(jnp.int32)
    l_high, l_low = _halves(local.astype(jnp.float32))
    values = jnp.concatenate(
        [marks * v.astype(jnp.float32) for v in (w_high, w_low, l_high, l_low)], axis=0
    ).astype(jnp.bfloat16)
    at = ((_iota((2 * slots, rows), 0) % slots) == place).astype(jnp.bfloat16)
    notes = _dot_t(values, at)
    weight = notes[:peers] + notes[peers : 2 * peers]
    index = notes[2 * peers : 3 * peers] + notes[3 * peers :]
    notes = jnp.where(first != odd_ref[0], weight, index)
    slot = target * slots + place
    block = 8
    for b in range(0, peers, block):
        take = (_iota((block * slots, rows), 0) + b * slots == slot).astype(jnp.bfloat16)
        got = _dot(take, both)
        got = got[:, :LANES] + got[:, LANES:]
        for t in range(block):
            base = (b + t) * (slots + 1)
            out_ref[base : base + slots, :] = got[t * slots : (t + 1) * slots]
            out_ref[base + slots : base + slots + 1, :] = notes[b + t : b + t + 1]


def _pack(points, weight, labels, odd, peers, slots, held):
    return pl.pallas_call(
        functools.partial(_pack_kernel, peers, slots, held),
        out_shape=jax.ShapeDtypeStruct((peers * (slots + 1), LANES), jnp.float32),
        in_specs=[pl.BlockSpec(memory_space=pltpu.SMEM)] + [pl.BlockSpec(memory_space=pltpu.VMEM)] * 3,
        compiler_params=pltpu.CompilerParams(vmem_limit_bytes=LIMIT),
        name="pack",
    )(odd, points, weight, labels)


def _repack_kernel(peers, slots, held, groups, shift_ref, x_ref, *refs):
    out_refs, (even_ref, odd_ref, both_ref) = refs[:-3], refs[-3:]
    pairs = peers // 2
    rows = peers * slots
    per = held // groups
    first = _iota((pairs, LANES), 1) < slots
    for b in range(peers):
        base = b * (slots + 1)
        high, low = _halves(x_ref[base : base + slots, :])
        both_ref[b * slots : (b + 1) * slots, :LANES] = high
        both_ref[b * slots : (b + 1) * slots, LANES:] = low
        note_ref = odd_ref if b % 2 else even_ref
        note_ref[b // 2 : b // 2 + 1, :] = x_ref[base + slots : base + slots + 1, :]
    even, odd = even_ref[...], odd_ref[...]
    weight = jnp.where(first, even, odd)
    local = pltpu.roll(jnp.where(first, odd, even), slots, 1).astype(jnp.int32)
    owner = local // per - shift_ref[0]
    owner = jnp.where(owner < 0, owner + groups, owner)
    owner = jnp.where(weight > 0.0, owner, -1)
    index = (local % per).astype(jnp.float32)
    marks = [
        (_iota((groups, LANES), 0) == owner[k : k + 1]).astype(jnp.float32) for k in range(pairs)
    ]
    places, sizes = _places(marks, groups)
    flag = jnp.max(sizes, axis=0, keepdims=True) > CAP
    flag = jnp.where(flag, jnp.ones((1, LANES), jnp.float32), 0.0)
    place = jnp.concatenate(places, axis=1).astype(jnp.int32)
    owner = jnp.concatenate([owner[k : k + 1] for k in range(pairs)], axis=1)
    fits = (owner >= 0) & (place < CAP)
    place = jnp.where(fits, place, -1)
    slot = jnp.where(fits, owner * PITCH + place, -1)
    w_high, w_low = _halves(weight)
    values = jnp.concatenate(
        [
            jnp.concatenate([marks[k] * v[k : k + 1] for k in range(pairs)], axis=1)
            for v in (w_high.astype(jnp.float32), w_low.astype(jnp.float32), index)
        ],
        axis=0,
    ).astype(jnp.bfloat16)
    at = (_iota((2 * LANES, rows), 0) == place).astype(jnp.bfloat16)
    notes = _dot_t(values, at)
    weight = notes[:groups] + notes[groups : 2 * groups]
    index = notes[2 * groups :]
    both = both_ref[...]
    for o in range(0, groups, 2):
        take = (_iota((2 * PITCH, rows), 0) + o * PITCH == slot).astype(jnp.bfloat16)
        got = _dot(take, both)
        got = got[:, :LANES] + got[:, LANES:]
        for half in range(2):
            own = o + half
            out_ref, base = (out_refs[own], 0) if len(out_refs) > 1 else (out_refs[0], own * PITCH)
            out_ref[base : base + PITCH, :] = got[half * PITCH : (half + 1) * PITCH]
            base = base + CAP
            out_ref[base : base + 1, :] = weight[own : own + 1, :LANES]
            out_ref[base + 1 : base + 2, :] = weight[own : own + 1, LANES:]
            out_ref[base + 2 : base + 3, :] = index[own : own + 1, :LANES]
            out_ref[base + 3 : base + 4, :] = index[own : own + 1, LANES:]
            out_ref[base + 4 : base + 5, :] = flag


def _repack(got, shift, parts, peers, slots, held, groups):
    return pl.pallas_call(
        functools.partial(_repack_kernel, peers, slots, held, groups),
        out_shape=[jax.ShapeDtypeStruct((groups // parts * PITCH, LANES), jnp.float32)] * parts,
        in_specs=[pl.BlockSpec(memory_space=pltpu.SMEM), pl.BlockSpec(memory_space=pltpu.VMEM)],
        scratch_shapes=[
            pltpu.VMEM((peers // 2, LANES), jnp.float32),
            pltpu.VMEM((peers // 2, LANES), jnp.float32),
            pltpu.VMEM((peers * slots, 2 * LANES), jnp.bfloat16),
        ],
        compiler_params=pltpu.CompilerParams(vmem_limit_bytes=LIMIT),
        name="repack",
    )(shift, got)


def _solve_kernel(groups, cur_ref, prior_ref, seen_ref, *refs):
    x_refs, (out_ref, flag_ref, high_ref, low_ref) = refs[:-4], refs[-4:]
    wide = 2 * LANES
    per = cur_ref.shape[0]
    ones = jnp.ones((8, LANES), jnp.bfloat16)
    flag = seen_ref[...]
    current = cur_ref[...]
    weights, indices, powers = [], [], []
    for s in range(groups):
        x_ref, base = (x_refs[s], 0) if len(x_refs) > 1 else (x_refs[0], s * PITCH)
        rows = x_ref[base : base + CAP, :]
        rows = jnp.concatenate([rows, jnp.zeros((wide - CAP, LANES), jnp.float32)], axis=0)
        high, low = _halves(rows)
        high_ref[s * wide : (s + 1) * wide, :] = high
        low_ref[s * wide : (s + 1) * wide, :] = low
        square_high, square_low = _halves(rows * rows)
        powers.append((_dot_t(ones, square_high) + _dot_t(ones, square_low))[:1])
        notes = x_ref[base + CAP : base + PITCH, :]
        weights += [notes[0:1], notes[1:2]]
        indices += [notes[2:3], notes[3:4]]
        flag = jnp.maximum(flag, notes[4:5])
    weight = jnp.concatenate(weights, axis=1)
    index = jnp.concatenate(indices, axis=1).astype(jnp.int32)
    power = jnp.concatenate(powers, axis=1) * (1.0 / LANES)
    coupling = weight * (parallel_ratio - 1.0) / (LANES * (power + tiny))
    mine = _iota((per, groups * wide), 0) == index
    weighted = jnp.where(mine, weight, 0.0)
    coupled = jnp.where(mine, coupling, 0.0)
    weight_sum = jnp.sum(weighted, axis=1, keepdims=True)
    high, low = high_ref[...], low_ref[...]

    def gather_up(terms):
        a, b = _halves(terms)
        c = _dot(jnp.concatenate([a, b], axis=0), high)
        return c[:per] + c[per:] + _dot(a, low)

    def along(vector):
        a, b = _halves(vector)
        c = _dot_t(jnp.concatenate([a, b], axis=0), high)
        return c[:per] + c[per:] + _dot_t(a, low)

    diagonal = prior_ref[...] + weight_sum
    rhs = prior_ref[...] * current + parallel_ratio * gather_up(weighted)
    current = jnp.zeros_like(rhs)
    residual = rhs
    direction = rhs
    norm_now = jnp.sum(residual * residual, axis=1, keepdims=True)
    for turn in range(ITERS):
        image = diagonal * direction + gather_up(along(direction) * coupled)
        alpha = norm_now / (jnp.sum(direction * image, axis=1, keepdims=True) + tiny)
        current = current + alpha * direction
        if turn + 1 < ITERS:
            residual = residual - alpha * image
            norm_next = jnp.sum(residual * residual, axis=1, keepdims=True)
            direction = residual + (norm_next / (norm_now + tiny)) * direction
            norm_now = norm_next
    out_ref[...] = current
    flag_ref[...] = flag


def _solve(got, current, prior, seen, groups):
    rows = groups * 2 * LANES
    return pl.pallas_call(
        functools.partial(_solve_kernel, groups),
        out_shape=(
            jax.ShapeDtypeStruct(current.shape, jnp.float32),
            jax.ShapeDtypeStruct((1, LANES), jnp.float32),
        ),
        scratch_shapes=[
            pltpu.VMEM((rows, LANES), jnp.bfloat16),
            pltpu.VMEM((rows, LANES), jnp.bfloat16),
        ],
        compiler_params=pltpu.CompilerParams(vmem_limit_bytes=LIMIT),
        name="solve",
    )(current, prior, seen, *got)


def row_terms(vector, got_points, got_weight, got_local, coupling, held):
    picked = jnp.take(vector, got_local, axis=0)
    along = jnp.sum(got_points * picked, axis=1) * coupling
    term = got_weight[:, None] * picked + along[:, None] * got_points
    return jax.ops.segment_sum(term, got_local, num_segments=held)


def dp_sum(x):
    groups = lax.axis_size("dp")
    parts = x.reshape(groups, -1, x.shape[1])
    parts = lax.all_to_all(parts, "dp", split_axis=0, concat_axis=0, tiled=True)
    spread = jnp.broadcast_to(jnp.sum(parts, axis=0)[None], parts.shape)
    return lax.all_to_all(spread, "dp", split_axis=0, concat_axis=0, tiled=True).reshape(x.shape)


def solve_whole(got_points, got_weight, got_local, coupling, current, prior_prec, held):
    data = jax.ops.segment_sum(got_weight[:, None] * got_points, got_local, num_segments=held)
    rhs = prior_prec[None, :] * current + parallel_ratio * dp_sum(data)
    solution = jnp.zeros_like(rhs)
    residual = rhs
    direction = rhs
    norm_now = jnp.sum(residual * residual, axis=1)
    for turn in range(ITERS):
        partial_value = row_terms(direction, got_points, got_weight, got_local, coupling, held)
        image = prior_prec[None, :] * direction + dp_sum(partial_value)
        alpha = norm_now / (jnp.sum(direction * image, axis=1) + tiny)
        solution = solution + alpha[:, None] * direction
        residual = residual - alpha[:, None] * image
        norm_next = jnp.sum(residual * residual, axis=1)
        direction = residual + (norm_next / (norm_now + tiny))[:, None] * direction
        norm_now = norm_next
    return solution


def any_labels(got, centroids, prior_prec, peers, slots):
    held, width = centroids.shape
    current = centroids
    for block in got:
        block = block.reshape(peers, slots + 1, width)
        points = block[:, :slots].reshape(-1, width)
        notes = block[:, slots].reshape(peers // 2, 2, 2, slots)
        weight = jnp.stack([notes[:, 0, 0], notes[:, 1, 1]], axis=1).reshape(-1)
        local = jnp.stack([notes[:, 0, 1], notes[:, 1, 0]], axis=1).reshape(-1).astype(jnp.int32)
        power = jnp.mean(points * points, axis=1)
        coupling = weight * (parallel_ratio - 1.0) / (width * (power + tiny))
        current = solve_whole(points, weight, local, coupling, current, prior_prec, held)
    return current


def per_device(points, row_weight, labels, centroids, prior_prec):
    peers = lax.axis_size("cent")
    groups = lax.axis_size("dp")
    held, width = centroids.shape
    slots = 2 * points.shape[0] // peers
    steps = labels.shape[0]
    per = held // groups
    odd = (lax.axis_index("cent") % 2).reshape(1)
    mine = lax.axis_index("dp")
    start = mine * per
    weight, prior = row_weight.reshape(1, -1), prior_prec.reshape(1, -1)
    got = []
    for step in range(steps):
        sent = _pack(points, weight, labels[step : step + 1], odd, peers, slots, held)
        if got:
            sent, got[-1] = lax.optimization_barrier((sent, got[-1]))
        sent = sent.reshape(peers, slots + 1, 1, width)
        block = lax.all_to_all(sent, "cent", split_axis=0, concat_axis=0, tiled=True)
        got.append(block.reshape(-1, width))
    current = lax.dynamic_slice(centroids, (start, 0), (per, width))
    flag = jnp.zeros((1, LANES), jnp.float32)
    for step in range(steps):
        if step + 1 < steps:
            again = list(_repack(got[step], mine.reshape(1), groups, peers, slots, held, groups))
            for k in range(1, groups):
                again[k] = lax.ppermute(again[k], "dp", [(i, (i + k) % groups) for i in range(groups)])
            again, got[step + 1] = lax.optimization_barrier((again, got[step + 1]))
        else:
            again = _repack(got[step], jnp.zeros((1,), jnp.int32), 1, peers, slots, held, groups)[0]
            again = again.reshape(groups, PITCH, width)
            again = lax.all_to_all(again, "dp", split_axis=0, concat_axis=0, tiled=True)
            again = [again.reshape(-1, width)]
        current, flag = _solve(again, current, prior, flag, groups)

    def summed(got, current):
        every = any_labels(got, centroids, prior_prec, peers, slots)
        return lax.dynamic_slice(every, (start, 0), (per, width))

    current = lax.cond(flag[0, 0] > 0.0, summed, lambda got, current: current, got, current)
    spread = jnp.broadcast_to(current[None], (groups, per, width))
    spread = lax.all_to_all(spread, "dp", split_axis=0, concat_axis=0, tiled=True)
    return spread.reshape(held, width)


def solution(mesh):
    in_specs = (
        P(("dp", "cent"), None),
        P(("dp", "cent")),
        P(None, ("dp", "cent")),
        P("cent", None),
        P(),
    )
    out_specs = P("cent", None)
    return jax.shard_map(
        per_device, mesh=mesh, in_specs=in_specs, out_specs=out_specs, check_vma=False
    )
```

```python
import functools
import math

import jax
import jax.numpy as jnp
from jax import lax
from jax.experimental import pallas as pl
from jax.experimental.pallas import tpu as pltpu
from jax.sharding import PartitionSpec as P

ITERS = 3
CAP = 168
HALF = 80
PITCH = CAP + 8
LANES = 128
LIMIT = 24 * 1024 * 1024

parallel_ratio = 4.0
tiny = 1e-06


def _dot(a, b):
    return jnp.dot(a, b, preferred_element_type=jnp.float32)


def _dot_t(a, b):
    return lax.dot_general(a, b, (((1,), (1,)), ((), ())), preferred_element_type=jnp.float32)


def _halves(x):
    high = x.astype(jnp.bfloat16)
    low = (x - high.astype(jnp.float32)).astype(jnp.bfloat16)
    return high, low


def _iota(shape, dim):
    return lax.broadcasted_iota(jnp.int32, shape, dim)


def _ramp(rows, columns):
    return _iota((rows, columns), 0).astype(jnp.float32).astype(jnp.bfloat16)


def _hits(ramp, places):
    return jnp.where(ramp == places.astype(jnp.bfloat16), jnp.ones_like(ramp), jnp.zeros_like(ramp))


def _upper():
    return (_iota((LANES, LANES), 0) <= _iota((LANES, LANES), 1)).astype(jnp.bfloat16)


def _places(marks, groups):
    within = _dot(jnp.concatenate(marks, axis=0).astype(jnp.bfloat16), _upper())
    before = jnp.zeros((groups, 1), jnp.float32)
    places = []
    for k, mark in enumerate(marks):
        part = within[k * groups : (k + 1) * groups]
        places.append(jnp.sum(mark * (part + (before - 1.0)), axis=0, keepdims=True))
        before = before + part[:, LANES - 1 :]
    return places, before


def _pack_kernel(peers, slots, held, odd_ref, x_ref, w_ref, t_ref, out_ref):
    rows = x_ref.shape[0]
    high, low = _halves(x_ref[...])
    both = jnp.concatenate([high, low], axis=1)
    w_high, w_low = _halves(w_ref[...])
    first = (_iota((peers, 2 * slots), 1) < slots).astype(jnp.int32)
    label = t_ref[...]
    target = label // held
    local = label - target * held
    marks = (_iota((peers, rows), 0) == target).astype(jnp.float32)
    chunks = [marks[:, k : k + LANES] for k in range(0, rows, LANES)]
    places, _ = _places(chunks, peers)
    place = jnp.concatenate(places, axis=1)
    l_high, l_low = _halves(local.astype(jnp.float32))
    values = jnp.concatenate(
        [marks * v.astype(jnp.float32) for v in (w_high, w_low, l_high, l_low)], axis=0
    ).astype(jnp.bfloat16)
    ramp = _ramp(slots, rows)
    at = _hits(ramp, place)
    at = jnp.concatenate([at, at], axis=0)
    notes = _dot_t(values, at)
    weight = notes[:peers] + notes[peers : 2 * peers]
    index = notes[2 * peers : 3 * peers] + notes[3 * peers :]
    notes = jnp.where(first != odd_ref[0], weight, index)
    placed = jnp.where(marks > 0.0, place, -1.0)
    block = 8
    for b in range(0, peers, block):
        take = jnp.concatenate([_hits(ramp, placed[t : t + 1]) for t in range(b, b + block)], axis=0)
        got = _dot(take, both)
        got = got[:, :LANES] + got[:, LANES:]
        for t in range(block):
            base = (b + t) * (slots + 1)
            out_ref[base : base + slots, :] = got[t * slots : (t + 1) * slots]
            out_ref[base + slots : base + slots + 1, :] = notes[b + t : b + t + 1]


def _pack(points, weight, labels, odd, peers, slots, held):
    return pl.pallas_call(
        functools.partial(_pack_kernel, peers, slots, held),
        out_shape=jax.ShapeDtypeStruct((peers * (slots + 1), LANES), jnp.float32),
        in_specs=[pl.BlockSpec(memory_space=pltpu.SMEM)] + [pl.BlockSpec(memory_space=pltpu.VMEM)] * 3,
        compiler_params=pltpu.CompilerParams(vmem_limit_bytes=LIMIT),
        name="pack",
    )(odd, points, weight, labels)


def _sources(groups):
    side = math.isqrt(groups)
    table = []
    for k in range(side):
        for j in range(side):
            one = (k, 0, HALF) if j == 0 else (side + j - 1, k * HALF, HALF)
            two = (2 * side - 1 + j, 0) if k == 0 else (3 * side - 2 + k, j * (PITCH - HALF))
            table.append(((one, two + (CAP - HALF,)), (two[0], two[1] + CAP - HALF)))
    return tuple(table)


def _repack_kernel(peers, slots, held, groups, me_ref, x_ref, *refs):
    out_refs, (even_ref, odd_ref, both_ref) = refs[:-3], refs[-3:]
    side = math.isqrt(groups)
    pairs = peers // 2
    rows = peers * slots
    per = held // groups
    first = _iota((pairs, LANES), 1) < slots
    for b in range(peers):
        base = b * (slots + 1)
        high, low = _halves(x_ref[base : base + slots, :])
        both_ref[b * slots : (b + 1) * slots, :LANES] = high
        both_ref[b * slots : (b + 1) * slots, LANES:] = low
        note_ref = odd_ref if b % 2 else even_ref
        note_ref[b // 2 : b // 2 + 1, :] = x_ref[base + slots : base + slots + 1, :]
    even, odd = even_ref[...], odd_ref[...]
    weight = jnp.where(first, even, odd)
    local = pltpu.roll(jnp.where(first, odd, even), slots, 1).astype(jnp.int32)
    owner = local // per
    if len(out_refs) > 1:
        far_x = owner % side - me_ref[0] % side
        far_y = owner // side - me_ref[0] // side
        far_x = jnp.where(far_x < 0, far_x + side, far_x)
        far_y = jnp.where(far_y < 0, far_y + side, far_y)
        owner = far_x * side + far_y
    owner = jnp.where(weight > 0.0, owner, -1)
    index = (local % per).astype(jnp.float32)
    marks = [
        (_iota((groups, LANES), 0) == owner[k : k + 1]).astype(jnp.float32) for k in range(pairs)
    ]
    places, sizes = _places(marks, groups)
    flag = jnp.max(sizes, axis=0, keepdims=True) > CAP
    flag = jnp.where(flag, jnp.ones((1, LANES), jnp.float32), 0.0)
    place = jnp.concatenate(places, axis=1)
    place = jnp.where(place < CAP, place, -1.0)
    marks = jnp.concatenate(marks, axis=1)
    placed = jnp.where(marks > 0.0, place, -1.0)
    w_high, w_low = _halves(weight)
    values = jnp.concatenate(
        [
            marks * jnp.concatenate([v[k : k + 1] for k in range(pairs)], axis=1)
            for v in (w_high.astype(jnp.float32), w_low.astype(jnp.float32), index)
        ],
        axis=0,
    ).astype(jnp.bfloat16)
    ramp = _ramp(2 * LANES, rows)
    at = _hits(ramp, place)
    notes = _dot_t(values, at)
    weight = notes[:groups] + notes[groups : 2 * groups]
    index = notes[2 * groups :]
    both = both_ref[...]
    for o in range(0, groups, 2):
        take = [_hits(ramp[:PITCH], placed[i : i + 1]) for i in range(o, o + 2)]
        take = jnp.concatenate(take, axis=0)
        got = _dot(take, both)
        got = got[:, :LANES] + got[:, LANES:]
        for half in range(2):
            own = o + half
            rows_of = got[half * PITCH : (half + 1) * PITCH]
            if len(out_refs) > 1:
                k, j = own // side, own % side
                out_refs[k][j * HALF : (j + 1) * HALF, :] = rows_of[:HALF]
                out_ref, base = out_refs[side + j], k * (PITCH - HALF)
                out_ref[base : base + PITCH - HALF, :] = rows_of[HALF:]
                base = base + CAP - HALF
            else:
                out_ref, base = out_refs[0], own * PITCH
                out_ref[base : base + PITCH, :] = rows_of
                base = base + CAP
            out_ref[base : base + 1, :] = weight[own : own + 1, :LANES]
            out_ref[base + 1 : base + 2, :] = weight[own : own + 1, LANES:]
            out_ref[base + 2 : base + 3, :] = index[own : own + 1, :LANES]
            out_ref[base + 3 : base + 4, :] = index[own : own + 1, LANES:]
            out_ref[base + 4 : base + 5, :] = flag


def _repack(got, me, split, peers, slots, held, groups):
    side = math.isqrt(groups)
    shapes = [side * HALF] * side + [side * (PITCH - HALF)] * side if split else [groups * PITCH]
    return pl.pallas_call(
        functools.partial(_repack_kernel, peers, slots, held, groups),
        out_shape=[jax.ShapeDtypeStruct((rows, LANES), jnp.float32) for rows in shapes],
        in_specs=[pl.BlockSpec(memory_space=pltpu.SMEM), pl.BlockSpec(memory_space=pltpu.VMEM)],
        scratch_shapes=[
            pltpu.VMEM((peers // 2, LANES), jnp.float32),
            pltpu.VMEM((peers // 2, LANES), jnp.float32),
            pltpu.VMEM((peers * slots, 2 * LANES), jnp.bfloat16),
        ],
        compiler_params=pltpu.CompilerParams(vmem_limit_bytes=LIMIT),
        name="repack",
    )(me, got)


def _solve_kernel(table, cur_ref, prior_ref, seen_ref, *refs):
    x_refs, (out_ref, flag_ref, both_ref) = refs[:-3], refs[-3:]
    wide = 2 * LANES
    per = cur_ref.shape[0]
    ones = jnp.ones((8, 2 * LANES), jnp.bfloat16)
    flag = seen_ref[...]
    current = cur_ref[...]
    weights, indices, powers = [], [], []
    groups = len(table)
    for s, (parts, (note, first)) in enumerate(table):
        rows = [x_refs[ref][base : base + count, :] for ref, base, count in parts]
        rows = jnp.concatenate(rows + [jnp.zeros((wide - CAP, LANES), jnp.float32)], axis=0)
        high, low = _halves(rows)
        both_ref[s * wide : (s + 1) * wide, :LANES] = high
        both_ref[s * wide : (s + 1) * wide, LANES:] = low
        powers.append(_dot_t(ones, jnp.concatenate(_halves(rows * rows), axis=1))[:1])
        notes = x_refs[note][first : first + PITCH - CAP, :]
        weights += [notes[0:1], notes[1:2]]
        indices += [notes[2:3], notes[3:4]]
        flag = jnp.maximum(flag, notes[4:5])
    weight = jnp.concatenate(weights, axis=1)
    index = jnp.concatenate(indices, axis=1).astype(jnp.int32)
    power = jnp.concatenate(powers, axis=1) * (1.0 / LANES)
    coupling = weight * (parallel_ratio - 1.0) / (LANES * (power + tiny))
    mine = _iota((per, groups * wide), 0) == index
    weighted = jnp.where(mine, weight, 0.0)
    coupled = jnp.where(mine, coupling, 0.0)
    weight_sum = jnp.sum(weighted, axis=1, keepdims=True)
    both = both_ref[...]

    def gather_up(terms):
        c = _dot(jnp.concatenate(_halves(terms), axis=0), both)
        c = c[:, :LANES] + c[:, LANES:]
        return c[:per] + c[per:]

    def along(vector):
        c = jnp.concatenate(_halves(vector), axis=0)
        c = _dot_t(jnp.concatenate([c, c], axis=1), both)
        return c[:per] + c[per:]

    diagonal = prior_ref[...] + weight_sum
    rhs = prior_ref[...] * current + parallel_ratio * gather_up(weighted)
    current = jnp.zeros_like(rhs)
    residual = rhs
    direction = rhs
    norm_now = jnp.sum(residual * residual, axis=1, keepdims=True)
    for turn in range(ITERS):
        image = diagonal * direction + gather_up(along(direction) * coupled)
        alpha = norm_now / (jnp.sum(direction * image, axis=1, keepdims=True) + tiny)
        current = current + alpha * direction
        if turn + 1 < ITERS:
            residual = residual - alpha * image
            norm_next = jnp.sum(residual * residual, axis=1, keepdims=True)
            direction = residual + (norm_next / (norm_now + tiny)) * direction
            norm_now = norm_next
    out_ref[...] = current
    flag_ref[...] = flag


def _solve(got, current, prior, seen, table):
    rows = len(table) * 2 * LANES
    return pl.pallas_call(
        functools.partial(_solve_kernel, table),
        out_shape=(
            jax.ShapeDtypeStruct(current.shape, jnp.float32),
            jax.ShapeDtypeStruct((1, LANES), jnp.float32),
        ),
        scratch_shapes=[
            pltpu.VMEM((rows, 2 * LANES), jnp.bfloat16),
        ],
        compiler_params=pltpu.CompilerParams(vmem_limit_bytes=LIMIT),
        name="solve",
    )(current, prior, seen, *got)


def row_terms(vector, got_points, got_weight, got_local, coupling, held):
    picked = jnp.take(vector, got_local, axis=0)
    along = jnp.sum(got_points * picked, axis=1) * coupling
    term = got_weight[:, None] * picked + along[:, None] * got_points
    return jax.ops.segment_sum(term, got_local, num_segments=held)


def dp_sum(x):
    groups = lax.axis_size("dp")
    parts = x.reshape(groups, -1, x.shape[1])
    parts = lax.all_to_all(parts, "dp", split_axis=0, concat_axis=0, tiled=True)
    spread = jnp.broadcast_to(jnp.sum(parts, axis=0)[None], parts.shape)
    return lax.all_to_all(spread, "dp", split_axis=0, concat_axis=0, tiled=True).reshape(x.shape)


def solve_whole(got_points, got_weight, got_local, coupling, current, prior_prec, held):
    data = jax.ops.segment_sum(got_weight[:, None] * got_points, got_local, num_segments=held)
    rhs = prior_prec[None, :] * current + parallel_ratio * dp_sum(data)
    solution = jnp.zeros_like(rhs)
    residual = rhs
    direction = rhs
    norm_now = jnp.sum(residual * residual, axis=1)
    for turn in range(ITERS):
        partial_value = row_terms(direction, got_points, got_weight, got_local, coupling, held)
        image = prior_prec[None, :] * direction + dp_sum(partial_value)
        alpha = norm_now / (jnp.sum(direction * image, axis=1) + tiny)
        solution = solution + alpha[:, None] * direction
        residual = residual - alpha[:, None] * image
        norm_next = jnp.sum(residual * residual, axis=1)
        direction = residual + (norm_next / (norm_now + tiny))[:, None] * direction
        norm_now = norm_next
    return solution


def any_labels(got, centroids, prior_prec, peers, slots):
    held, width = centroids.shape
    current = centroids
    for block in got:
        block = block.reshape(peers, slots + 1, width)
        points = block[:, :slots].reshape(-1, width)
        notes = block[:, slots].reshape(peers // 2, 2, 2, slots)
        weight = jnp.stack([notes[:, 0, 0], notes[:, 1, 1]], axis=1).reshape(-1)
        local = jnp.stack([notes[:, 0, 1], notes[:, 1, 0]], axis=1).reshape(-1).astype(jnp.int32)
        power = jnp.mean(points * points, axis=1)
        coupling = weight * (parallel_ratio - 1.0) / (width * (power + tiny))
        current = solve_whole(points, weight, local, coupling, current, prior_prec, held)
    return current


def _spread(blocks, groups):
    side = math.isqrt(groups)

    def move(x, k, along_x):
        def to(i):
            y, x = divmod(i, side)
            return y * side + (x + k) % side if along_x else (y + k) % side * side + x

        return lax.ppermute(x, "dp", [(i, to(i)) for i in range(groups)]) if k else x

    first, second = blocks[:side], blocks[side:]
    once_1, once_2 = [first[0]], [second[0]]
    for k in range(1, side):
        once_1.append(move(first[k], k, True))
        once_2.append(move(second[k], k, False))
    twice_1, twice_2 = [], []
    for k in range(1, side):
        a, b = k * HALF, k * (PITCH - HALF)
        both = jnp.concatenate([x[a : a + HALF] for x in once_1], axis=0)
        twice_1.append(move(both, k, False))
        both = jnp.concatenate([x[b : b + PITCH - HALF] for x in once_2], axis=0)
        twice_2.append(move(both, k, True))
    return once_1 + twice_1 + once_2 + twice_2


def per_device(points, row_weight, labels, centroids, prior_prec):
    peers = lax.axis_size("cent")
    groups = lax.axis_size("dp")
    held, width = centroids.shape
    slots = 2 * points.shape[0] // peers
    steps = labels.shape[0]
    per = held // groups
    odd = (lax.axis_index("cent") % 2).reshape(1)
    mine = lax.axis_index("dp")
    start = mine * per
    weight, prior = row_weight.reshape(1, -1), prior_prec.reshape(1, -1)
    got = []
    for step in range(steps):
        sent = _pack(points, weight, labels[step : step + 1], odd, peers, slots, held)
        if got:
            sent, got[-1] = lax.optimization_barrier((sent, got[-1]))
        sent = sent.reshape(peers, slots + 1, 1, width)
        block = lax.all_to_all(sent, "cent", split_axis=0, concat_axis=0, tiled=True)
        got.append(block.reshape(-1, width))
    current = lax.dynamic_slice(centroids, (start, 0), (per, width))
    flag = jnp.zeros((1, LANES), jnp.float32)
    args = peers, slots, held, groups
    for step in range(steps):
        if step + 1 < steps:
            again = _spread(_repack(got[step], mine.reshape(1), True, *args), groups)
            again, got[step + 1] = lax.optimization_barrier((again, got[step + 1]))
            table = _sources(groups)
        else:
            again = _repack(got[step], mine.reshape(1), False, *args)[0].reshape(groups, PITCH, width)
            again = lax.all_to_all(again, "dp", split_axis=0, concat_axis=0, tiled=True)
            again = [again.reshape(-1, width)]
            table = tuple((((0, s * PITCH, CAP),), (0, s * PITCH + CAP)) for s in range(groups))
        current, flag = _solve(again, current, prior, flag, table)

    def summed(got, current):
        every = any_labels(got, centroids, prior_prec, peers, slots)
        return lax.dynamic_slice(every, (start, 0), (per, width))

    current = lax.cond(flag[0, 0] > 0.0, summed, lambda got, current: current, got, current)
    spread = jnp.broadcast_to(current[None], (groups, per, width))
    spread = lax.all_to_all(spread, "dp", split_axis=0, concat_axis=0, tiled=True)
    return spread.reshape(held, width)


def solution(mesh):
    in_specs = (
        P(("dp", "cent"), None),
        P(("dp", "cent")),
        P(None, ("dp", "cent")),
        P("cent", None),
        P(),
    )
    out_specs = P("cent", None)
    return jax.shard_map(
        per_device, mesh=mesh, in_specs=in_specs, out_specs=out_specs, check_vma=False
    )
```

```python
import functools
import math

import jax
import jax.numpy as jnp
from jax import lax
from jax.experimental import pallas as pl
from jax.experimental.pallas import tpu as pltpu
from jax.sharding import PartitionSpec as P

ITERS = 3
FIRST = (168, 176, 80)
EARLY = (112, 120, 56)
LATE = (89, 92, 0)
LANES = 128
LIMIT = 24 * 1024 * 1024

parallel_ratio = 4.0
tiny = 1e-06


def _dot(a, b):
    return jnp.dot(a, b, preferred_element_type=jnp.float32)


def _dot_t(a, b):
    return lax.dot_general(a, b, (((1,), (1,)), ((), ())), preferred_element_type=jnp.float32)


def _halves(x):
    high = x.astype(jnp.bfloat16)
    low = (x - high.astype(jnp.float32)).astype(jnp.bfloat16)
    return high, low


def _iota(shape, dim):
    return lax.broadcasted_iota(jnp.int32, shape, dim)


def _ramp(rows, columns):
    return _iota((rows, columns), 0).astype(jnp.float32).astype(jnp.bfloat16)


def _hits(ramp, places):
    return jnp.where(ramp == places.astype(jnp.bfloat16), jnp.ones_like(ramp), jnp.zeros_like(ramp))


def _upper():
    return (_iota((LANES, LANES), 0) <= _iota((LANES, LANES), 1)).astype(jnp.bfloat16)


def _places(marks, groups):
    within = _dot(jnp.concatenate(marks, axis=0).astype(jnp.bfloat16), _upper())
    before = jnp.zeros((groups, 1), jnp.float32)
    places = []
    for k, mark in enumerate(marks):
        part = within[k * groups : (k + 1) * groups]
        places.append(jnp.sum(mark * (part + (before - 1.0)), axis=0, keepdims=True))
        before = before + part[:, LANES - 1 :]
    return places, before


def _pack_kernel(peers, slots, held, odd_ref, x_ref, w_ref, t_ref, out_ref):
    rows = x_ref.shape[0]
    high, low = _halves(x_ref[...])
    both = jnp.concatenate([high, low], axis=1)
    w_high, w_low = _halves(w_ref[...])
    first = (_iota((peers, 2 * slots), 1) < slots).astype(jnp.int32)
    label = t_ref[...]
    target = label // held
    local = label - target * held
    marks = (_iota((peers, rows), 0) == target).astype(jnp.float32)
    chunks = [marks[:, k : k + LANES] for k in range(0, rows, LANES)]
    places, _ = _places(chunks, peers)
    place = jnp.concatenate(places, axis=1)
    l_high, l_low = _halves(local.astype(jnp.float32))
    values = jnp.concatenate(
        [marks * v.astype(jnp.float32) for v in (w_high, w_low, l_high, l_low)], axis=0
    ).astype(jnp.bfloat16)
    ramp = _ramp(slots, rows)
    at = _hits(ramp, place)
    at = jnp.concatenate([at, at], axis=0)
    notes = _dot_t(values, at)
    weight = notes[:peers] + notes[peers : 2 * peers]
    index = notes[2 * peers : 3 * peers] + notes[3 * peers :]
    notes = jnp.where(first != odd_ref[0], weight, index)
    placed = jnp.where(marks > 0.0, place, -1.0)
    block = 8
    for b in range(0, peers, block):
        take = jnp.concatenate([_hits(ramp, placed[t : t + 1]) for t in range(b, b + block)], axis=0)
        got = _dot(take, both)
        got = got[:, :LANES] + got[:, LANES:]
        for t in range(block):
            base = (b + t) * (slots + 1)
            out_ref[base : base + slots, :] = got[t * slots : (t + 1) * slots]
            out_ref[base + slots : base + slots + 1, :] = notes[b + t : b + t + 1]


def _pack(points, weight, labels, odd, peers, slots, held):
    return pl.pallas_call(
        functools.partial(_pack_kernel, peers, slots, held),
        out_shape=jax.ShapeDtypeStruct((peers * (slots + 1), LANES), jnp.float32),
        in_specs=[pl.BlockSpec(memory_space=pltpu.SMEM)] + [pl.BlockSpec(memory_space=pltpu.VMEM)] * 3,
        compiler_params=pltpu.CompilerParams(vmem_limit_bytes=LIMIT),
        name="pack",
    )(odd, points, weight, labels)


def _sources(groups, form):
    cap, pitch, half = form
    side = math.isqrt(groups)
    table = []
    for k in range(side):
        for j in range(side):
            one = (k, 0, half) if j == 0 else (side + j - 1, k * half, half)
            two = (2 * side - 1 + j, 0) if k == 0 else (3 * side - 2 + k, j * (pitch - half))
            table.append(((one, two + (cap - half,)), (two[0], two[1] + cap - half)))
    return tuple(table)


def _whole(sources, form):
    cap, pitch, _ = form
    return tuple((((0, s * pitch, pitch),), (0, s * pitch + cap)) for s in range(sources))


def _distance(owner, me, side):
    far_x = owner % side - me % side
    far_y = owner // side - me // side
    far_x = jnp.where(far_x < 0, far_x + side, far_x)
    far_y = jnp.where(far_y < 0, far_y + side, far_y)
    return far_x * side + far_y


def _deal(weights, owners, indices, both, groups, form, seen, out_refs):
    cap, pitch, half = form
    side = math.isqrt(groups)
    rows = LANES * len(owners)
    marks = [(_iota((groups, LANES), 0) == owner).astype(jnp.float32) for owner in owners]
    places, sizes = _places(marks, groups)
    flag = jnp.max(sizes, axis=0, keepdims=True) > cap
    flag = jnp.maximum(seen, jnp.where(flag, jnp.ones((1, LANES), jnp.float32), 0.0))
    place = jnp.concatenate(places, axis=1)
    place = jnp.where(place < cap, place, -1.0)
    marks = jnp.concatenate(marks, axis=1)
    placed = jnp.where(marks > 0.0, place, -1.0)
    terms = _halves(jnp.concatenate(weights, axis=1)) + _halves(jnp.concatenate(indices, axis=1))
    values = jnp.concatenate([marks * v.astype(jnp.float32) for v in terms], axis=0).astype(jnp.bfloat16)
    wide = -(-cap // LANES) * LANES
    ramp = _ramp(max(wide, pitch), rows)
    notes = _dot_t(values, _hits(ramp[:wide], place))
    weight = notes[:groups] + notes[groups : 2 * groups]
    index = notes[2 * groups : 3 * groups] + notes[3 * groups :]
    tall = -(-pitch // 16) * 16
    for first in range(0, groups, 4):
        take = [_hits(ramp[:tall], placed[o : o + 1]) for o in range(first, first + 4)]
        got = _dot(jnp.concatenate(take, axis=0), both)
        got = got[:, :LANES] + got[:, LANES:]
        for o in range(first, first + 4):
            block = got[(o - first) * tall : (o - first) * tall + pitch]
            if half:
                k, j = o // side, o % side
                out_refs[k][j * half : (j + 1) * half, :] = block[:half]
                out_ref, base = out_refs[side + j], k * (pitch - half)
            else:
                out_ref, base = out_refs[0], o * pitch
            out_ref[base : base + pitch - half, :] = block[half:]
            base = base + cap - half
            own = [v[o : o + 1, c : c + LANES] for v in (weight, index) for c in range(0, wide, LANES)]
            for n, note in enumerate(own + [flag]):
                out_ref[base + n : base + n + 1, :] = note


def _blocks(groups, form):
    _, pitch, half = form
    side = math.isqrt(groups)
    heights = [side * half] * side + [side * (pitch - half)] * side if half else [groups * pitch]
    return [jax.ShapeDtypeStruct((rows, LANES), jnp.float32) for rows in heights]


def _repack_kernel(peers, slots, held, groups, me_ref, x_ref, *refs):
    out_refs, (even_ref, odd_ref, both_ref) = refs[:-3], refs[-3:]
    pairs = peers // 2
    per = held // groups
    first = _iota((pairs, LANES), 1) < slots
    for b in range(peers):
        base = b * (slots + 1)
        high, low = _halves(x_ref[base : base + slots, :])
        both_ref[b * slots : (b + 1) * slots, :LANES] = high
        both_ref[b * slots : (b + 1) * slots, LANES:] = low
        note_ref = odd_ref if b % 2 else even_ref
        note_ref[b // 2 : b // 2 + 1, :] = x_ref[base + slots : base + slots + 1, :]
    even, odd = even_ref[...], odd_ref[...]
    weight = jnp.where(first, even, odd)
    local = pltpu.roll(jnp.where(first, odd, even), slots, 1).astype(jnp.int32)
    owner = _distance(local // per, me_ref[0], math.isqrt(groups))
    owner = jnp.where(weight > 0.0, owner, -1)
    index = (local % per).astype(jnp.float32)
    split = [[v[k : k + 1] for k in range(pairs)] for v in (weight, owner, index)]
    _deal(*split, both_ref[...], groups, FIRST, jnp.zeros((1, LANES), jnp.float32), out_refs)


def _repack(got, me, peers, slots, held, groups):
    return pl.pallas_call(
        functools.partial(_repack_kernel, peers, slots, held, groups),
        out_shape=_blocks(groups, FIRST),
        in_specs=[pl.BlockSpec(memory_space=pltpu.SMEM), pl.BlockSpec(memory_space=pltpu.VMEM)],
        scratch_shapes=[
            pltpu.VMEM((peers // 2, LANES), jnp.float32),
            pltpu.VMEM((peers // 2, LANES), jnp.float32),
            pltpu.VMEM((peers * slots, 2 * LANES), jnp.bfloat16),
        ],
        compiler_params=pltpu.CompilerParams(vmem_limit_bytes=LIMIT),
        name="repack",
    )(me, got)


def _early_kernel(held, groups, me_ref, x_ref, w_ref, t_ref, *out_refs):
    rows = x_ref.shape[0]
    per = held // groups
    label = t_ref[...]
    local = label % held
    owner = _distance(local // per, me_ref[0], math.isqrt(groups))
    index = (label // held * per + local % per).astype(jnp.float32)
    both = jnp.concatenate(_halves(x_ref[...]), axis=1)
    split = [[v[:, k : k + LANES] for k in range(0, rows, LANES)] for v in (w_ref[...], owner, index)]
    _deal(*split, both, groups, EARLY, jnp.zeros((1, LANES), jnp.float32), out_refs)


def _early(points, weight, labels, me, held, groups):
    return pl.pallas_call(
        functools.partial(_early_kernel, held, groups),
        out_shape=_blocks(groups, EARLY),
        in_specs=[pl.BlockSpec(memory_space=pltpu.SMEM)] + [pl.BlockSpec(memory_space=pltpu.VMEM)] * 3,
        compiler_params=pltpu.CompilerParams(vmem_limit_bytes=LIMIT),
        name="early",
    )(me, points, weight, labels)


def _late_kernel(table, peers, per, *refs):
    x_refs, (out_ref, both_ref) = refs[:-2], refs[-2:]
    weights, owners, indices = [], [], []
    flag = jnp.zeros((1, LANES), jnp.float32)
    for s, (parts, (note, first)) in enumerate(table):
        rows = [x_refs[ref][base : base + count, :] for ref, base, count in parts]
        filled = sum(count for _, _, count in parts)
        rows = jnp.concatenate(rows + [jnp.zeros((LANES - filled, LANES), jnp.float32)], axis=0)
        high, low = _halves(rows)
        both_ref[s * LANES : (s + 1) * LANES, :LANES] = high
        both_ref[s * LANES : (s + 1) * LANES, LANES:] = low
        notes = x_refs[note][first : first + 8, :]
        index = notes[1:2].astype(jnp.int32)
        weights.append(notes[0:1])
        owners.append(jnp.where(notes[0:1] > 0.0, index // per, -1))
        indices.append((index % per).astype(jnp.float32))
        flag = jnp.maximum(flag, notes[2:3])
    _deal(weights, owners, indices, both_ref[...], peers, LATE, flag, [out_ref])


def _late(early, table, peers, per):
    return pl.pallas_call(
        functools.partial(_late_kernel, table, peers, per),
        out_shape=_blocks(peers, LATE)[0],
        scratch_shapes=[pltpu.VMEM((len(table) * LANES, 2 * LANES), jnp.bfloat16)],
        compiler_params=pltpu.CompilerParams(vmem_limit_bytes=LIMIT),
        name="late",
    )(*early)


def _solve_kernel(table, wide, per, cur_ref, prior_ref, *refs):
    x_refs, (out_ref, both_ref) = refs[:-2], refs[-2:]
    count = wide // LANES
    ones = jnp.ones((8, 2 * LANES), jnp.bfloat16)
    flag = jnp.zeros((1, LANES), jnp.float32)
    current = cur_ref[:per, :]
    weights, indices, powers = [], [], []
    groups = len(table)
    for s, (parts, (note, first)) in enumerate(table):
        rows = [x_refs[ref][base : base + tall, :] for ref, base, tall in parts]
        filled = sum(tall for _, _, tall in parts)
        rows = jnp.concatenate(rows + [jnp.zeros((wide - filled, LANES), jnp.float32)], axis=0)
        high, low = _halves(rows)
        both_ref[s * wide : (s + 1) * wide, :LANES] = high
        both_ref[s * wide : (s + 1) * wide, LANES:] = low
        powers.append(_dot_t(ones, jnp.concatenate(_halves(rows * rows), axis=1))[:1])
        notes = x_refs[note][first : first + 2 * count + 1, :]
        weights += [notes[n : n + 1] for n in range(count)]
        indices += [notes[n : n + 1] for n in range(count, 2 * count)]
        flag = jnp.maximum(flag, notes[2 * count :])
    weight = jnp.concatenate(weights, axis=1)
    index = jnp.concatenate(indices, axis=1).astype(jnp.int32)
    power = jnp.concatenate(powers, axis=1) * (1.0 / LANES)
    coupling = weight * (parallel_ratio - 1.0) / (LANES * (power + tiny))
    mine = _iota((per, groups * wide), 0) == index
    weighted = jnp.where(mine, weight, 0.0)
    coupled = jnp.where(mine, coupling, 0.0)
    weight_sum = jnp.sum(weighted, axis=1, keepdims=True)
    both = both_ref[...]

    def gather_up(terms):
        c = _dot(jnp.concatenate(_halves(terms), axis=0), both)
        c = c[:, :LANES] + c[:, LANES:]
        return c[:per] + c[per:]

    def along(vector):
        c = jnp.concatenate(_halves(vector), axis=0)
        c = _dot_t(jnp.concatenate([c, c], axis=1), both)
        return c[:per] + c[per:]

    diagonal = prior_ref[...] + weight_sum
    rhs = prior_ref[...] * current + parallel_ratio * gather_up(weighted)
    current = jnp.zeros_like(rhs)
    residual = rhs
    direction = rhs
    norm_now = jnp.sum(residual * residual, axis=1, keepdims=True)
    for turn in range(ITERS):
        image = diagonal * direction + gather_up(along(direction) * coupled)
        alpha = norm_now / (jnp.sum(direction * image, axis=1, keepdims=True) + tiny)
        current = current + alpha * direction
        if turn + 1 < ITERS:
            residual = residual - alpha * image
            norm_next = jnp.sum(residual * residual, axis=1, keepdims=True)
            direction = residual + (norm_next / (norm_now + tiny)) * direction
            norm_now = norm_next
    out_ref[:per, :] = current
    out_ref[per:, :] = jnp.zeros((8, LANES), jnp.float32) + flag


def _solve(got, current, prior, table, wide, per):
    return pl.pallas_call(
        functools.partial(_solve_kernel, table, wide, per),
        out_shape=jax.ShapeDtypeStruct((per + 8, LANES), jnp.float32),
        scratch_shapes=[pltpu.VMEM((len(table) * wide, 2 * LANES), jnp.bfloat16)],
        compiler_params=pltpu.CompilerParams(vmem_limit_bytes=LIMIT),
        name="solve",
    )(current, prior, *got)


def row_terms(vector, got_points, got_weight, got_local, coupling, held):
    picked = jnp.take(vector, got_local, axis=0)
    along = jnp.sum(got_points * picked, axis=1) * coupling
    term = got_weight[:, None] * picked + along[:, None] * got_points
    return jax.ops.segment_sum(term, got_local, num_segments=held)


def dp_sum(x):
    groups = lax.axis_size("dp")
    parts = x.reshape(groups, -1, x.shape[1])
    parts = lax.all_to_all(parts, "dp", split_axis=0, concat_axis=0, tiled=True)
    spread = jnp.broadcast_to(jnp.sum(parts, axis=0)[None], parts.shape)
    return lax.all_to_all(spread, "dp", split_axis=0, concat_axis=0, tiled=True).reshape(x.shape)


def solve_whole(got_points, got_weight, got_local, coupling, current, prior_prec, held):
    data = jax.ops.segment_sum(got_weight[:, None] * got_points, got_local, num_segments=held)
    rhs = prior_prec[None, :] * current + parallel_ratio * dp_sum(data)
    solution = jnp.zeros_like(rhs)
    residual = rhs
    direction = rhs
    norm_now = jnp.sum(residual * residual, axis=1)
    for turn in range(ITERS):
        partial_value = row_terms(direction, got_points, got_weight, got_local, coupling, held)
        image = prior_prec[None, :] * direction + dp_sum(partial_value)
        alpha = norm_now / (jnp.sum(direction * image, axis=1) + tiny)
        solution = solution + alpha[:, None] * direction
        residual = residual - alpha[:, None] * image
        norm_next = jnp.sum(residual * residual, axis=1)
        direction = residual + (norm_next / (norm_now + tiny))[:, None] * direction
        norm_now = norm_next
    return solution


def any_labels(got, centroids, prior_prec, peers, slots):
    held, width = centroids.shape
    current = centroids
    for block in got:
        block = block.reshape(peers, slots + 1, width)
        points = block[:, :slots].reshape(-1, width)
        notes = block[:, slots].reshape(peers // 2, 2, 2, slots)
        weight = jnp.stack([notes[:, 0, 0], notes[:, 1, 1]], axis=1).reshape(-1)
        local = jnp.stack([notes[:, 0, 1], notes[:, 1, 0]], axis=1).reshape(-1).astype(jnp.int32)
        power = jnp.mean(points * points, axis=1)
        coupling = weight * (parallel_ratio - 1.0) / (width * (power + tiny))
        current = solve_whole(points, weight, local, coupling, current, prior_prec, held)
    return current


def _spread(blocks, groups, form):
    side = math.isqrt(groups)

    def move(x, k, along_x):
        def to(i):
            y, x = divmod(i, side)
            return y * side + (x + k) % side if along_x else (y + k) % side * side + x

        return lax.ppermute(x, "dp", [(i, to(i)) for i in range(groups)]) if k else x

    _, pitch, half = form
    first, second = blocks[:side], blocks[side:]
    once_1, once_2 = [first[0]], [second[0]]
    for k in range(1, side):
        once_1.append(move(first[k], k, True))
        once_2.append(move(second[k], k, False))
    twice_1, twice_2 = [], []
    for k in range(1, side):
        a, b = k * half, k * (pitch - half)
        both = jnp.concatenate([x[a : a + half] for x in once_1], axis=0)
        twice_1.append(move(both, k, False))
        both = jnp.concatenate([x[b : b + pitch - half] for x in once_2], axis=0)
        twice_2.append(move(both, k, True))
    return once_1 + twice_1 + once_2 + twice_2


def per_device(points, row_weight, labels, centroids, prior_prec):
    peers = lax.axis_size("cent")
    groups = lax.axis_size("dp")
    held, width = centroids.shape
    slots = 2 * points.shape[0] // peers
    per = held // groups
    odd = (lax.axis_index("cent") % 2).reshape(1)
    mine = lax.axis_index("dp")
    start = mine * per
    weight, prior = row_weight.reshape(1, -1), prior_prec.reshape(1, -1)

    def fetch(sent):
        block = sent.reshape(peers, -1, 1, width)
        return lax.all_to_all(block, "cent", split_axis=0, concat_axis=0, tiled=True).reshape(-1, width)

    sent = _pack(points, weight, labels[:1], odd, peers, slots, held)
    sent, second = lax.optimization_barrier((sent, labels[1:]))
    got = fetch(sent)
    early = _spread(_early(points, weight, second, mine.reshape(1), held, groups), groups, EARLY)
    late = _late(early, _sources(groups, EARLY), peers, per)
    late, got = lax.optimization_barrier((late, got))
    late = fetch(late)
    again = _spread(_repack(got, mine.reshape(1), peers, slots, held, groups), groups, FIRST)
    current = lax.dynamic_slice(centroids, (start, 0), (per, width))
    state = _solve(again, current, prior, _sources(groups, FIRST), 2 * LANES, per)
    state, late = lax.optimization_barrier((state, late))

    def summed(got, state):
        every = any_labels([got], centroids, prior_prec, peers, slots)
        every = lax.dynamic_slice(every, (start, 0), (per, width))
        return jnp.concatenate([every, jnp.zeros((8, width), jnp.float32)], axis=0)

    state = lax.cond(state[per, 0] > 0.0, summed, lambda got, state: state, got, state)
    state = _solve([late], state, prior, _whole(peers, LATE), LANES, per)
    spread = jnp.broadcast_to(state[None], (groups, per + 8, width))
    spread = lax.all_to_all(spread, "dp", split_axis=0, concat_axis=0, tiled=True)

    def every_step(spread):
        got = [
            fetch(_pack(points, weight, labels[s : s + 1], odd, peers, slots, held))
            for s in range(labels.shape[0])
        ]
        return any_labels(got, centroids, prior_prec, peers, slots)

    return lax.cond(
        jnp.max(spread[:, per, 0]) > 0.0,
        every_step,
        lambda spread: spread[:, :per].reshape(held, width),
        spread,
    )


def solution(mesh):
    in_specs = (
        P(("dp", "cent"), None),
        P(("dp", "cent")),
        P(None, ("dp", "cent")),
        P("cent", None),
        P(),
    )
    out_specs = P("cent", None)
    return jax.shard_map(
        per_device, mesh=mesh, in_specs=in_specs, out_specs=out_specs, check_vma=False
    )
```

```python
import functools
import math

import jax
import jax.numpy as jnp
from jax import lax
from jax.experimental import pallas as pl
from jax.experimental.pallas import tpu as pltpu
from jax.sharding import PartitionSpec as P

ITERS = 3
FIRST = (168, 176, 80)
EARLY = (112, 120, 56)
LATE = (89, 92, 0)
LANES = 128
LIMIT = 24 * 1024 * 1024

parallel_ratio = 4.0
tiny = 1e-06


def _dot(a, b):
    return jnp.dot(a, b, preferred_element_type=jnp.float32)


def _dot_t(a, b):
    return lax.dot_general(a, b, (((1,), (1,)), ((), ())), preferred_element_type=jnp.float32)


def _halves(x):
    high = x.astype(jnp.bfloat16)
    low = (x - high.astype(jnp.float32)).astype(jnp.bfloat16)
    return high, low


def _iota(shape, dim):
    return lax.broadcasted_iota(jnp.int32, shape, dim)


def _ramp(rows, columns):
    return _iota((rows, columns), 0).astype(jnp.float32).astype(jnp.bfloat16)


def _hits(ramp, places):
    return jnp.where(ramp == places.astype(jnp.bfloat16), jnp.ones_like(ramp), jnp.zeros_like(ramp))


def _upper():
    return (_iota((LANES, LANES), 0) <= _iota((LANES, LANES), 1)).astype(jnp.bfloat16)


def _places(marks, groups):
    within = _dot(jnp.concatenate(marks, axis=0).astype(jnp.bfloat16), _upper())
    before = jnp.zeros((groups, 1), jnp.float32)
    places = []
    for k, mark in enumerate(marks):
        part = within[k * groups : (k + 1) * groups]
        places.append(jnp.sum(mark * (part + (before - 1.0)), axis=0, keepdims=True))
        before = before + part[:, LANES - 1 :]
    return places, before


def _pack_kernel(peers, slots, held, odd_ref, x_ref, w_ref, t_ref, out_ref):
    rows = x_ref.shape[0]
    high, low = _halves(x_ref[...])
    both = jnp.concatenate([high, low], axis=1)
    w_high, w_low = _halves(w_ref[...])
    first = (_iota((peers, 2 * slots), 1) < slots).astype(jnp.int32)
    label = t_ref[...]
    target = label // held
    local = label - target * held
    marks = (_iota((peers, rows), 0) == target).astype(jnp.float32)
    chunks = [marks[:, k : k + LANES] for k in range(0, rows, LANES)]
    places, _ = _places(chunks, peers)
    place = jnp.concatenate(places, axis=1)
    l_high, l_low = _halves(local.astype(jnp.float32))
    values = jnp.concatenate(
        [marks * v.astype(jnp.float32) for v in (w_high, w_low, l_high, l_low)], axis=0
    ).astype(jnp.bfloat16)
    ramp = _ramp(slots, rows)
    at = _hits(ramp, place)
    at = jnp.concatenate([at, at], axis=0)
    notes = _dot_t(values, at)
    weight = notes[:peers] + notes[peers : 2 * peers]
    index = notes[2 * peers : 3 * peers] + notes[3 * peers :]
    notes = jnp.where(first != odd_ref[0], weight, index)
    placed = jnp.where(marks > 0.0, place, -1.0)
    block = 8
    for b in range(0, peers, block):
        take = jnp.concatenate([_hits(ramp, placed[t : t + 1]) for t in range(b, b + block)], axis=0)
        got = _dot(take, both)
        got = got[:, :LANES] + got[:, LANES:]
        for t in range(block):
            base = (b + t) * (slots + 1)
            out_ref[base : base + slots, :] = got[t * slots : (t + 1) * slots]
            out_ref[base + slots : base + slots + 1, :] = notes[b + t : b + t + 1]


def _pack(points, weight, labels, odd, peers, slots, held):
    return pl.pallas_call(
        functools.partial(_pack_kernel, peers, slots, held),
        out_shape=jax.ShapeDtypeStruct((peers * (slots + 1), LANES), jnp.float32),
        in_specs=[pl.BlockSpec(memory_space=pltpu.SMEM)] + [pl.BlockSpec(memory_space=pltpu.VMEM)] * 3,
        compiler_params=pltpu.CompilerParams(vmem_limit_bytes=LIMIT),
        name="pack",
    )(odd, points, weight, labels)


def _sources(groups, form):
    cap, pitch, half = form
    side = math.isqrt(groups)
    table = []
    for k in range(side):
        for j in range(side):
            one = (k, 0, half) if j == 0 else (side + j - 1, k * half, half)
            two = (2 * side - 1 + j, 0) if k == 0 else (3 * side - 2 + k, j * (pitch - half))
            table.append(((one, two + (cap - half,)), (two[0], two[1] + cap - half)))
    return tuple(table)


def _whole(sources, form):
    cap, pitch, _ = form
    return tuple((((0, s * pitch, pitch),), (0, s * pitch + cap)) for s in range(sources))


def _distance(owner, me, side):
    far_x = owner % side - me % side
    far_y = owner // side - me // side
    far_x = jnp.where(far_x < 0, far_x + side, far_x)
    far_y = jnp.where(far_y < 0, far_y + side, far_y)
    return far_x * side + far_y


def _deal(weights, owners, indices, both, groups, form, seen, out_refs):
    cap, pitch, half = form
    side = math.isqrt(groups)
    rows = LANES * len(owners)
    marks = [(_iota((groups, LANES), 0) == owner).astype(jnp.float32) for owner in owners]
    places, sizes = _places(marks, groups)
    flag = jnp.max(sizes, axis=0, keepdims=True) > cap
    flag = jnp.maximum(seen, jnp.where(flag, jnp.ones((1, LANES), jnp.float32), 0.0))
    place = jnp.concatenate(places, axis=1)
    place = jnp.where(place < cap, place, -1.0)
    marks = jnp.concatenate(marks, axis=1)
    placed = jnp.where(marks > 0.0, place, -1.0)
    terms = _halves(jnp.concatenate(weights, axis=1)) + _halves(jnp.concatenate(indices, axis=1))
    values = jnp.concatenate([marks * v.astype(jnp.float32) for v in terms], axis=0).astype(jnp.bfloat16)
    wide = -(-cap // LANES) * LANES
    ramp = _ramp(max(wide, pitch), rows)
    notes = _dot_t(values, _hits(ramp[:wide], place))
    weight = notes[:groups] + notes[groups : 2 * groups]
    index = notes[2 * groups : 3 * groups] + notes[3 * groups :]
    tall = -(-pitch // 16) * 16
    for first in range(0, groups, 4):
        take = [_hits(ramp[:tall], placed[o : o + 1]) for o in range(first, first + 4)]
        got = _dot(jnp.concatenate(take, axis=0), both)
        got = got[:, :LANES] + got[:, LANES:]
        for o in range(first, first + 4):
            block = got[(o - first) * tall : (o - first) * tall + pitch]
            if half:
                k, j = o // side, o % side
                out_refs[k][j * half : (j + 1) * half, :] = block[:half]
                out_ref, base = out_refs[side + j], k * (pitch - half)
            else:
                out_ref, base = out_refs[0], o * pitch
            out_ref[base : base + pitch - half, :] = block[half:]
            base = base + cap - half
            own = [v[o : o + 1, c : c + LANES] for v in (weight, index) for c in range(0, wide, LANES)]
            for n, note in enumerate(own + [flag]):
                out_ref[base + n : base + n + 1, :] = note


def _blocks(groups, form):
    _, pitch, half = form
    side = math.isqrt(groups)
    heights = [side * half] * side + [side * (pitch - half)] * side if half else [groups * pitch]
    return [jax.ShapeDtypeStruct((rows, LANES), jnp.float32) for rows in heights]


def _repack_kernel(peers, slots, held, groups, me_ref, x_ref, *refs):
    out_refs, (even_ref, odd_ref, both_ref) = refs[:-3], refs[-3:]
    pairs = peers // 2
    per = held // groups
    first = _iota((pairs, LANES), 1) < slots
    for b in range(peers):
        base = b * (slots + 1)
        high, low = _halves(x_ref[base : base + slots, :])
        both_ref[b * slots : (b + 1) * slots, :LANES] = high
        both_ref[b * slots : (b + 1) * slots, LANES:] = low
        note_ref = odd_ref if b % 2 else even_ref
        note_ref[b // 2 : b // 2 + 1, :] = x_ref[base + slots : base + slots + 1, :]
    even, odd = even_ref[...], odd_ref[...]
    weight = jnp.where(first, even, odd)
    local = pltpu.roll(jnp.where(first, odd, even), slots, 1).astype(jnp.int32)
    owner = _distance(local // per, me_ref[0], math.isqrt(groups))
    owner = jnp.where(weight > 0.0, owner, -1)
    index = (local % per).astype(jnp.float32)
    split = [[v[k : k + 1] for k in range(pairs)] for v in (weight, owner, index)]
    _deal(*split, both_ref[...], groups, FIRST, jnp.zeros((1, LANES), jnp.float32), out_refs)


def _repack(got, me, peers, slots, held, groups):
    return pl.pallas_call(
        functools.partial(_repack_kernel, peers, slots, held, groups),
        out_shape=_blocks(groups, FIRST),
        in_specs=[pl.BlockSpec(memory_space=pltpu.SMEM), pl.BlockSpec(memory_space=pltpu.VMEM)],
        scratch_shapes=[
            pltpu.VMEM((peers // 2, LANES), jnp.float32),
            pltpu.VMEM((peers // 2, LANES), jnp.float32),
            pltpu.VMEM((peers * slots, 2 * LANES), jnp.bfloat16),
        ],
        compiler_params=pltpu.CompilerParams(vmem_limit_bytes=LIMIT),
        name="repack",
    )(me, got)


def _early_kernel(held, groups, me_ref, x_ref, w_ref, t_ref, *out_refs):
    rows = x_ref.shape[0]
    per = held // groups
    label = t_ref[...]
    local = label % held
    owner = _distance(local // per, me_ref[0], math.isqrt(groups))
    index = (label // held * per + local % per).astype(jnp.float32)
    both = jnp.concatenate(_halves(x_ref[...]), axis=1)
    split = [[v[:, k : k + LANES] for k in range(0, rows, LANES)] for v in (w_ref[...], owner, index)]
    _deal(*split, both, groups, EARLY, jnp.zeros((1, LANES), jnp.float32), out_refs)


def _early(points, weight, labels, me, held, groups):
    return pl.pallas_call(
        functools.partial(_early_kernel, held, groups),
        out_shape=_blocks(groups, EARLY),
        in_specs=[pl.BlockSpec(memory_space=pltpu.SMEM)] + [pl.BlockSpec(memory_space=pltpu.VMEM)] * 3,
        compiler_params=pltpu.CompilerParams(vmem_limit_bytes=LIMIT),
        name="early",
    )(me, points, weight, labels)


def _late_kernel(table, peers, per, *refs):
    x_refs, (out_ref, both_ref) = refs[:-2], refs[-2:]
    weights, owners, indices = [], [], []
    flag = jnp.zeros((1, LANES), jnp.float32)
    for s, (parts, (note, first)) in enumerate(table):
        rows = [x_refs[ref][base : base + count, :] for ref, base, count in parts]
        filled = sum(count for _, _, count in parts)
        rows = jnp.concatenate(rows + [jnp.zeros((LANES - filled, LANES), jnp.float32)], axis=0)
        high, low = _halves(rows)
        both_ref[s * LANES : (s + 1) * LANES, :LANES] = high
        both_ref[s * LANES : (s + 1) * LANES, LANES:] = low
        notes = x_refs[note][first : first + 8, :]
        index = notes[1:2].astype(jnp.int32)
        weights.append(notes[0:1])
        owners.append(jnp.where(notes[0:1] > 0.0, index // per, -1))
        indices.append((index % per).astype(jnp.float32))
        flag = jnp.maximum(flag, notes[2:3])
    _deal(weights, owners, indices, both_ref[...], peers, LATE, flag, [out_ref])


def _late(early, table, peers, per):
    return pl.pallas_call(
        functools.partial(_late_kernel, table, peers, per),
        out_shape=_blocks(peers, LATE)[0],
        scratch_shapes=[pltpu.VMEM((len(table) * LANES, 2 * LANES), jnp.bfloat16)],
        compiler_params=pltpu.CompilerParams(vmem_limit_bytes=LIMIT),
        name="late",
    )(*early)


def _solve_kernel(table, wide, per, cur_ref, prior_ref, *refs):
    x_refs, (out_ref, both_ref) = refs[:-2], refs[-2:]
    count = wide // LANES
    ones = jnp.ones((8, 2 * LANES), jnp.bfloat16)
    flag = jnp.zeros((1, LANES), jnp.float32)
    current = cur_ref[:per, :]
    weights, indices, powers = [], [], []
    groups = len(table)
    for s, (parts, (note, first)) in enumerate(table):
        rows = [x_refs[ref][base : base + tall, :] for ref, base, tall in parts]
        filled = sum(tall for _, _, tall in parts)
        rows = jnp.concatenate(rows + [jnp.zeros((wide - filled, LANES), jnp.float32)], axis=0)
        high, low = _halves(rows)
        both_ref[s * wide : (s + 1) * wide, :LANES] = high
        both_ref[s * wide : (s + 1) * wide, LANES:] = low
        powers.append(_dot_t(ones, jnp.concatenate(_halves(rows * rows), axis=1))[:1])
        notes = x_refs[note][first : first + 2 * count + 1, :]
        weights += [notes[n : n + 1] for n in range(count)]
        indices += [notes[n : n + 1] for n in range(count, 2 * count)]
        flag = jnp.maximum(flag, notes[2 * count :])
    weight = jnp.concatenate(weights, axis=1)
    index = jnp.concatenate(indices, axis=1).astype(jnp.int32)
    power = jnp.concatenate(powers, axis=1) * (1.0 / LANES)
    coupling = weight * (parallel_ratio - 1.0) / (LANES * (power + tiny))
    mine = _iota((per, groups * wide), 0) == index
    weighted = jnp.where(mine, weight, 0.0)
    coupled = jnp.where(mine, coupling, 0.0)
    weight_sum = jnp.sum(weighted, axis=1, keepdims=True)
    both = both_ref[...]

    def gather_up(terms):
        c = _dot(jnp.concatenate(_halves(terms), axis=0), both)
        c = c[:, :LANES] + c[:, LANES:]
        return c[:per] + c[per:]

    def along(vector):
        c = jnp.concatenate(_halves(vector), axis=0)
        c = _dot_t(jnp.concatenate([c, c], axis=1), both)
        return c[:per] + c[per:]

    diagonal = prior_ref[...] + weight_sum
    rhs = prior_ref[...] * current + parallel_ratio * gather_up(weighted)
    current = jnp.zeros_like(rhs)
    residual = rhs
    direction = rhs
    norm_now = jnp.sum(residual * residual, axis=1, keepdims=True)
    for turn in range(ITERS):
        image = diagonal * direction + gather_up(along(direction) * coupled)
        alpha = norm_now / (jnp.sum(direction * image, axis=1, keepdims=True) + tiny)
        current = current + alpha * direction
        if turn + 1 < ITERS:
            residual = residual - alpha * image
            norm_next = jnp.sum(residual * residual, axis=1, keepdims=True)
            direction = residual + (norm_next / (norm_now + tiny)) * direction
            norm_now = norm_next
    out_ref[:per, :] = current
    out_ref[per:, :] = jnp.zeros((8, LANES), jnp.float32) + flag


def _solve(got, current, prior, table, wide, per):
    return pl.pallas_call(
        functools.partial(_solve_kernel, table, wide, per),
        out_shape=jax.ShapeDtypeStruct((per + 8, LANES), jnp.float32),
        scratch_shapes=[pltpu.VMEM((len(table) * wide, 2 * LANES), jnp.bfloat16)],
        compiler_params=pltpu.CompilerParams(vmem_limit_bytes=LIMIT),
        name="solve",
    )(current, prior, *got)


def row_terms(vector, got_points, got_weight, got_local, coupling, held):
    picked = jnp.take(vector, got_local, axis=0)
    along = jnp.sum(got_points * picked, axis=1) * coupling
    term = got_weight[:, None] * picked + along[:, None] * got_points
    return jax.ops.segment_sum(term, got_local, num_segments=held)


def dp_sum(x):
    groups = lax.axis_size("dp")
    parts = x.reshape(groups, -1, x.shape[1])
    parts = lax.all_to_all(parts, "dp", split_axis=0, concat_axis=0, tiled=True)
    spread = jnp.broadcast_to(jnp.sum(parts, axis=0)[None], parts.shape)
    return lax.all_to_all(spread, "dp", split_axis=0, concat_axis=0, tiled=True).reshape(x.shape)


def solve_whole(got_points, got_weight, got_local, coupling, current, prior_prec, held):
    data = jax.ops.segment_sum(got_weight[:, None] * got_points, got_local, num_segments=held)
    rhs = prior_prec[None, :] * current + parallel_ratio * dp_sum(data)
    solution = jnp.zeros_like(rhs)
    residual = rhs
    direction = rhs
    norm_now = jnp.sum(residual * residual, axis=1)
    for turn in range(ITERS):
        partial_value = row_terms(direction, got_points, got_weight, got_local, coupling, held)
        image = prior_prec[None, :] * direction + dp_sum(partial_value)
        alpha = norm_now / (jnp.sum(direction * image, axis=1) + tiny)
        solution = solution + alpha[:, None] * direction
        residual = residual - alpha[:, None] * image
        norm_next = jnp.sum(residual * residual, axis=1)
        direction = residual + (norm_next / (norm_now + tiny))[:, None] * direction
        norm_now = norm_next
    return solution


def any_labels(got, centroids, prior_prec, peers, slots):
    held, width = centroids.shape
    current = centroids
    for block in got:
        block = block.reshape(peers, slots + 1, width)
        points = block[:, :slots].reshape(-1, width)
        notes = block[:, slots].reshape(peers // 2, 2, 2, slots)
        weight = jnp.stack([notes[:, 0, 0], notes[:, 1, 1]], axis=1).reshape(-1)
        local = jnp.stack([notes[:, 0, 1], notes[:, 1, 0]], axis=1).reshape(-1).astype(jnp.int32)
        power = jnp.mean(points * points, axis=1)
        coupling = weight * (parallel_ratio - 1.0) / (width * (power + tiny))
        current = solve_whole(points, weight, local, coupling, current, prior_prec, held)
    return current


def _spread(blocks, groups, form):
    side = math.isqrt(groups)

    def move(x, k, along_x):
        def to(i):
            y, x = divmod(i, side)
            return y * side + (x + k) % side if along_x else (y + k) % side * side + x

        return lax.ppermute(x, "dp", [(i, to(i)) for i in range(groups)]) if k else x

    _, pitch, half = form
    first, second = blocks[:side], blocks[side:]
    once_1, once_2 = [first[0]], [second[0]]
    for k in range(1, side):
        once_1.append(move(first[k], k, True))
        once_2.append(move(second[k], k, False))
    twice_1, twice_2 = [], []
    for k in range(1, side):
        a, b = k * half, k * (pitch - half)
        both = jnp.concatenate([x[a : a + half] for x in once_1], axis=0)
        twice_1.append(move(both, k, False))
        both = jnp.concatenate([x[b : b + pitch - half] for x in once_2], axis=0)
        twice_2.append(move(both, k, True))
    return once_1 + twice_1 + once_2 + twice_2


def per_device(points, row_weight, labels, centroids, prior_prec):
    peers = lax.axis_size("cent")
    groups = lax.axis_size("dp")
    held, width = centroids.shape
    slots = 2 * points.shape[0] // peers
    per = held // groups
    odd = (lax.axis_index("cent") % 2).reshape(1)
    mine = lax.axis_index("dp")
    start = mine * per
    weight, prior = row_weight.reshape(1, -1), prior_prec.reshape(1, -1)

    def fetch(sent):
        block = sent.reshape(peers, -1, 1, width)
        return lax.all_to_all(block, "cent", split_axis=0, concat_axis=0, tiled=True).reshape(-1, width)

    sent = _pack(points, weight, labels[:1], odd, peers, slots, held)
    sent, second = lax.optimization_barrier((sent, labels[1:]))
    got = fetch(sent)
    early = _spread(_early(points, weight, second, mine.reshape(1), held, groups), groups, EARLY)
    late = _late(early, _sources(groups, EARLY), peers, per)
    late, got = lax.optimization_barrier((late, got))
    late = fetch(late)
    again = _spread(_repack(got, mine.reshape(1), peers, slots, held, groups), groups, FIRST)
    current = lax.dynamic_slice(centroids, (start, 0), (per, width))
    state = _solve(again, current, prior, _sources(groups, FIRST), 2 * LANES, per)
    full = state[per, 0] > 0.0
    state, late = lax.optimization_barrier((state, late))

    def summed(got, state):
        every = any_labels([got], centroids, prior_prec, peers, slots)
        every = lax.dynamic_slice(every, (start, 0), (per, width))
        return jnp.concatenate([every, jnp.zeros((8, width), jnp.float32)], axis=0)

    state = lax.cond(full, summed, lambda got, state: state, got, state)
    state = _solve([late], state, prior, _whole(peers, LATE), LANES, per)
    spread = jnp.broadcast_to(state[None], (groups, per + 8, width))
    spread = lax.all_to_all(spread, "dp", split_axis=0, concat_axis=0, tiled=True)

    def every_step(spread):
        got = [
            fetch(_pack(points, weight, labels[s : s + 1], odd, peers, slots, held))
            for s in range(labels.shape[0])
        ]
        return any_labels(got, centroids, prior_prec, peers, slots)

    return lax.cond(
        jnp.max(spread[:, per, 0]) > 0.0,
        every_step,
        lambda spread: spread[:, :per].reshape(held, width),
        spread,
    )


def solution(mesh):
    in_specs = (
        P(("dp", "cent"), None),
        P(("dp", "cent")),
        P(None, ("dp", "cent")),
        P("cent", None),
        P(),
    )
    out_specs = P("cent", None)
    return jax.shard_map(
        per_device, mesh=mesh, in_specs=in_specs, out_specs=out_specs, check_vma=False
    )
```
